32 devices in a mesh: dp: 16 (over z, y, x), tensor: 2 (over core).
Axes of the slice: x: 2, y: 2, z: 4, core: 2. Of those that a mesh axis runs over, the one named last changes fastest.
Arguments:
- hidden: bfloat16 [2304, 4096], P(('dp', 'tensor')), may hold values from -6 to 6
- doc_ids: int32 [16, 144], replicated, may hold values from 0 to 3, never falling along the last dimension, each value on 1 to 72 neighbouring positions
- teacher: bfloat16 [2304, 8448], P('dp', 'tensor'), may hold values from -6 to 6
- rotation: int32 [1], replicated, may hold values from 0 to 15
- norm_gain_vector: float32 [4096], replicated, may hold values from 0.5 to 1.5
- proj_bias: float32 [8448], P('tensor'), may hold values from -3 to 3
- projection: bfloat16 [4096, 8448], P(None, 'tensor'), may hold values from -0.09375 to 0.09375
Outputs:
- hidden_gradient: bfloat16 [2304, 4096], P(('dp', 'tensor'))
- gain_gradient_mean: float32 [4096], replicated
- grad_bias: float32 [8448], P('tensor')
- distill_loss: float32 [], replicated
The draws below stay inside these ranges and needn't reach their ends.
Inputs may be any that keep to these rules, and one draw needn't show every extreme that they name: `doc_ids`: in each row the document numbers never fall; each document has 1 to 72 tokens and one has exactly 72.
All inputs are finite; a program needn't handle non-finite values.
Results may differ from the reference program's by a relative error of at most 0.0049.
The reference program's roundings to bfloat16 on the way count: a program that leaves them out, or rounds other values in their place, can miss the bound.
Values may be sent and summed in bfloat16 or wider, within the bound.
A program may use at most 128 MiB of HBM per device.

```python
import math
import jax
import jax.numpy as jnp
import numpy as np
from jax import lax

D = 4096
P_SIZE = 8448
TOK_DEV = 144
DOCS = 4
MOST_DOC = 72
TOKEN_TOTAL = 2304
N_DP = 16


def block_levels(own_key, shape, split, smallest, top_value):
    loudness, own = 1.0, jax.random.fold_in(own_key, 6)
    for axis_at, shards_of in split:
        heights = jnp.exp(jax.random.uniform(jax.random.fold_in(own, axis_at), (shards_of,), jnp.float32, smallest / len(split), top_value / len(split)))
        loudness = loudness * jnp.repeat(heights, shape[axis_at] // shards_of).reshape([-1 if axis == axis_at else 1 for axis in range(len(shape))])
    return loudness


def profile(amount, total, reach, lean):
    portions = [(1 << 20) // math.isqrt(rank ** lean) + 1 for rank in range(2, amount + 1)]
    surplus, holding = total - reach - (amount - 1), [1] * (amount - 1)
    while surplus > 0:
        movable = [i for i in range(amount - 1) if holding[i] < reach]
        whole, budget = sum([portions[i] for i in movable]), surplus
        for i in movable:
            more = min(reach - holding[i], max(1, budget * portions[i] // whole), surplus)
            holding[i] = holding[i] + more
            surplus = surplus - more
    return np.array([reach] + holding)


def uneven_parts(rng, number_of, total, most, slope):
    if number_of == 2:
        one = jax.random.randint(rng, (), max(1, total - most), min(most, total - 1) + 1)
        return jnp.stack([one, total - one])
    sizes = jnp.asarray(profile(number_of, total, most, slope), jnp.int32)
    pairs = (number_of - 1) // 2
    source_of, taker = sizes[1:1 + 2 * pairs:2], sizes[2:2 + 2 * pairs:2]
    margin = jnp.minimum(source_of - 1, most - taker)
    moved = jax.random.randint(jax.random.fold_in(rng, 1), (pairs,), 0, 1 << 20) % (margin + 1)
    sizes = sizes.at[1:1 + 2 * pairs:2].set(source_of - moved).at[2:2 + 2 * pairs:2].set(taker + moved)
    return sizes[jax.random.permutation(jax.random.fold_in(rng, 2), number_of)]


def centred(rng, extent, width, most, pieces=(), dtype=jnp.bfloat16):
    values = jax.random.normal(rng, extent, jnp.float32) * width
    if len(pieces) > 0:
        values = block_levels(rng, extent, pieces, -0.22, 0.18) * values
    return jnp.clip(values, min=-most, max=most).astype(dtype)


def setup_inputs(seed: int = 0) -> dict:
    key_of = jax.random.split(jax.random.key(seed), 8)
    hidden = centred(key_of[0], (TOKEN_TOTAL, D), 1.0, 6.0, ((0, 32),))
    doc_ids = jax.vmap(lambda own: jnp.searchsorted(jnp.cumsum(uneven_parts(own, DOCS, TOK_DEV, MOST_DOC, 2)), jnp.arange(TOK_DEV), side="right"))(jax.random.split(key_of[1], N_DP)).reshape((N_DP, TOK_DEV)).astype(jnp.int32)
    teacher = centred(key_of[2], (TOKEN_TOTAL, P_SIZE), 1.0, 6.0, ((0, 16), (1, 2)))
    rotation = jax.random.randint(key_of[3], (1,), 0, N_DP).astype(jnp.int32)
    norm_gain_vector = jnp.clip(1.0 + 0.1 * jax.random.normal(key_of[4], (D,), jnp.float32), 0.5, 1.5)
    proj_bias = centred(key_of[5], (P_SIZE,), 0.5, 3.0, ((0, 2),), jnp.float32)
    projection = centred(key_of[6], (D, P_SIZE), D ** -0.5, 0.09375, ((1, 2),))
    return dict(hidden=hidden, doc_ids=doc_ids, teacher=teacher, rotation=rotation, norm_gain_vector=norm_gain_vector, proj_bias=proj_bias, projection=projection)


norm_eps = 1e-05

def reference(hidden, doc_ids, teacher, rotation, norm_gain_vector, proj_bias, projection):
    value_entries = hidden.astype(jnp.float32)
    mean_sq = lax.optimization_barrier(jnp.mean(value_entries * value_entries, axis=-1, keepdims=True))
    inverse_root_mean = lax.rsqrt(mean_sq + norm_eps)
    unscaled_rows = value_entries * inverse_root_mean
    normalized_rows = (unscaled_rows * norm_gain_vector).astype(jnp.bfloat16)
    logits = jnp.dot(normalized_rows, projection, preferred_element_type=jnp.float32) + proj_bias
    shift_rows = (rotation[0] * TOK_DEV).astype(jnp.int32)
    target = jnp.roll(teacher, -shift_rows, axis=0).astype(jnp.float32)
    same_doc = lax.optimization_barrier(jnp.sum((doc_ids[:, :, None] == doc_ids[:, None, :]).astype(jnp.float32), axis=-1))
    weight = (TOK_DEV / (DOCS * same_doc)).reshape(-1)[:, None]
    error_rows = logits - target
    distill_loss = jnp.sum(weight * error_rows * error_rows) / (2.0 * TOKEN_TOTAL * P_SIZE)
    grad_out = (weight * error_rows).astype(jnp.bfloat16)
    grad_bias = lax.optimization_barrier(jnp.sum(grad_out.astype(jnp.float32), axis=0)) / TOKEN_TOTAL
    normalized_gradient = lax.dot_general(grad_out, projection, (((1,), (1,)), ((), ())), preferred_element_type=jnp.float32)
    gain_gradient_mean = lax.optimization_barrier(jnp.sum(normalized_gradient * unscaled_rows, axis=0)) / TOKEN_TOTAL
    unscaled_gradient = normalized_gradient * norm_gain_vector
    inner_product = lax.optimization_barrier(jnp.mean(unscaled_gradient * unscaled_rows, axis=-1, keepdims=True))
    hidden_gradient = (inverse_root_mean * (unscaled_gradient - unscaled_rows * inner_product)).astype(jnp.bfloat16)
    return (hidden_gradient, gain_gradient_mean, grad_bias, distill_loss)
```

```python
import functools

import jax
import jax.numpy as jnp
from jax import lax
from jax.experimental import pallas as pl
from jax.experimental.pallas import tpu as pltpu
from jax.sharding import PartitionSpec as P

DOCS = 4
norm_eps = 1e-05
LANES = 128
SUB = 8
MESH = pl.DeviceIdType.MESH
VMEM_LIMIT = 56 * 1024 * 1024
MOST_DIRECT = 16


def divisor_tile(width, most):
    units = width // LANES
    best = max(u for u in range(1, units + 1) if units % u == 0 and u * LANES <= most)
    return best * LANES


def logits_kernel(hid_ref, gain_ref, w_ref, b_ref, out_ref, normed):
    @pl.when(pl.program_id(0) == 0)
    def _():
        x = hid_ref[...].astype(jnp.float32)
        inv = lax.rsqrt(jnp.mean(x * x, axis=-1, keepdims=True) + norm_eps)
        normed[...] = ((x * inv) * gain_ref[...]).astype(jnp.bfloat16)

    out_ref[...] = (
        jnp.dot(normed[...], w_ref[...], preferred_element_type=jnp.float32) + b_ref[...]
    )


def logits_call(gathered, gain, projection, bias):
    rows, depth = gathered.shape
    cols = projection.shape[1]
    tile = divisor_tile(cols, 512)
    return pl.pallas_call(
        logits_kernel,
        grid=(cols // tile,),
        out_shape=jax.ShapeDtypeStruct((rows, cols), jnp.float32),
        in_specs=[
            pl.BlockSpec((rows, depth), lambda i: (0, 0)),
            pl.BlockSpec((1, depth), lambda i: (0, 0)),
            pl.BlockSpec((depth, tile), lambda i: (0, i)),
            pl.BlockSpec((1, tile), lambda i: (0, i)),
        ],
        out_specs=pl.BlockSpec((rows, tile), lambda i: (0, i)),
        scratch_shapes=[pltpu.VMEM((rows, depth), jnp.bfloat16)],
        cost_estimate=pl.CostEstimate(
            flops=2 * rows * depth * cols, bytes_accessed=2 * depth * cols, transcendentals=0
        ),
        compiler_params=pltpu.CompilerParams(vmem_limit_bytes=VMEM_LIMIT),
        name="logits",
    )(gathered, gain, projection, bias)


def grad_kernel(logit_ref, target_ref, weight_ref, w_ref, grad_ref, bias_ref, loss_ref):
    error = logit_ref[...] - target_ref[...].astype(jnp.float32)
    weighted = weight_ref[...] * error
    loss_ref[...] = jnp.sum(weighted * error, axis=0, keepdims=True)
    rounded = weighted.astype(jnp.bfloat16)
    bias_ref[...] = jnp.sum(rounded.astype(jnp.float32), axis=0, keepdims=True)
    part = lax.dot_general(
        rounded, w_ref[...], (((1,), (1,)), ((), ())), preferred_element_type=jnp.float32
    )

    @pl.when(pl.program_id(0) == 0)
    def _():
        grad_ref[...] = part

    @pl.when(pl.program_id(0) > 0)
    def _():
        grad_ref[...] += part


def grad_call(logits, target, weight, projection):
    rows, cols = logits.shape
    depth = projection.shape[0]
    tile = divisor_tile(cols, 512)
    return pl.pallas_call(
        grad_kernel,
        grid=(cols // tile,),
        out_shape=(
            jax.ShapeDtypeStruct((rows, depth), jnp.float32),
            jax.ShapeDtypeStruct((1, cols), jnp.float32),
            jax.ShapeDtypeStruct((1, cols), jnp.float32),
        ),
        in_specs=[
            pl.BlockSpec((rows, tile), lambda i: (0, i)),
            pl.BlockSpec((rows, tile), lambda i: (0, i)),
            pl.BlockSpec((rows, 1), lambda i: (0, 0)),
            pl.BlockSpec((depth, tile), lambda i: (0, i)),
        ],
        out_specs=(
            pl.BlockSpec((rows, depth), lambda i: (0, 0)),
            pl.BlockSpec((1, tile), lambda i: (0, i)),
            pl.BlockSpec((1, tile), lambda i: (0, i)),
        ),
        cost_estimate=pl.CostEstimate(
            flops=2 * rows * depth * cols, bytes_accessed=2 * depth * cols, transcendentals=0
        ),
        compiler_params=pltpu.CompilerParams(vmem_limit_bytes=VMEM_LIMIT),
        name="grads",
    )(logits, target, weight, projection)


def tail_kernel(
    n, teams, per, total_rows, loss_scale,
    grad_ref, full_ref, own_ref, gain_ref, bias_ref, loss_ref,
    hid_out, gain_out, bias_out, loss_out,
    got_grad, own_vec, got_vec, red, got_red, merged,
    gs, gr, ss, sr, ts, tr, bs, br,
):
    here = lax.axis_index("dp")
    core = lax.axis_index("tensor")
    portion = own_ref.shape[0]
    depth = full_ref.shape[1]
    cols = bias_ref.shape[1]
    gain_rows = depth // LANES
    bias_rows = cols // LANES

    barrier = pltpu.get_barrier_semaphore()

    def greet(step, carry):
        pl.semaphore_signal(
            barrier, inc=1, device_id=(lax.rem(here + step, n), core), device_id_type=MESH
        )
        return carry

    lax.fori_loop(1, n, greet, 0)
    for q in range(1, teams):
        pl.semaphore_signal(
            barrier, inc=1, device_id=(here, lax.rem(core + q, teams)), device_id_type=MESH
        )
    pl.semaphore_wait(barrier, n - 1 + teams - 1)

    def grad_copy(q):
        peer = lax.rem(core + q, teams)
        return pltpu.make_async_remote_copy(
            src_ref=grad_ref.at[pl.ds(pl.multiple_of(peer * portion, SUB), portion), :],
            dst_ref=got_grad.at[q - 1],
            send_sem=gs.at[q - 1],
            recv_sem=gr.at[q - 1],
            device_id=(here, peer),
            device_id_type=MESH,
        )

    for q in range(1, teams):
        grad_copy(q).start()

    x = full_ref[...].astype(jnp.float32)
    xhat = x * lax.rsqrt(jnp.mean(x * x, axis=-1, keepdims=True) + norm_eps)
    gain_part = jnp.sum(grad_ref[...] * xhat, axis=0, keepdims=True)
    loss_part = jnp.sum(loss_ref[...], axis=-1, keepdims=True)

    own_vec[...] = jnp.zeros_like(own_vec)
    for j in range(gain_rows):
        own_vec[j // per, pl.ds(j % per, 1), :] = gain_part[:, j * LANES:(j + 1) * LANES]
    j = gain_rows
    own_vec[j // per, pl.ds(j % per, 1), :] = jnp.broadcast_to(loss_part, (1, LANES))
    for i in range(bias_rows):
        j = gain_rows + 1 + i
        own_vec[j // per, pl.ds(j % per, 1), :] = bias_ref[:, i * LANES:(i + 1) * LANES]

    def scatter_copy(step):
        peer = lax.rem(here + step, n)
        return pltpu.make_async_remote_copy(
            src_ref=own_vec.at[peer],
            dst_ref=got_vec.at[step - 1],
            send_sem=ss.at[step - 1],
            recv_sem=sr.at[step - 1],
            device_id=(peer, core),
            device_id_type=MESH,
        )

    def scatter_start(step, carry):
        scatter_copy(step).start()
        return carry

    lax.fori_loop(1, n, scatter_start, 0)

    def scatter_wait(step, total):
        scatter_copy(step).wait()
        return total + got_vec[step - 1]

    red[...] = lax.fori_loop(1, n, scatter_wait, own_vec[here])

    def team_copy(q):
        peer = lax.rem(core + q, teams)
        return pltpu.make_async_remote_copy(
            src_ref=red,
            dst_ref=got_red.at[q - 1],
            send_sem=ts.at[q - 1],
            recv_sem=tr.at[q - 1],
            device_id=(here, peer),
            device_id_type=MESH,
        )

    for q in range(1, teams):
        team_copy(q).start()
    for q in range(1, teams):
        team_copy(q).wait()
    others = jnp.zeros(red.shape, jnp.float32)
    for q in range(1, teams):
        others = others + got_red[q - 1]
    row_at = here * per + lax.broadcasted_iota(jnp.int32, red.shape, 0)
    merged[here] = red[...] + jnp.where(row_at <= gain_rows, others, 0.0)

    def spread_copy(step):
        peer = lax.rem(here + step, n)
        return pltpu.make_async_remote_copy(
            src_ref=merged.at[here],
            dst_ref=merged.at[here],
            send_sem=bs.at[step - 1],
            recv_sem=br.at[step - 1],
            device_id=(peer, core),
            device_id_type=MESH,
        )

    def spread_start(step, carry):
        spread_copy(step).start()
        return carry

    lax.fori_loop(1, n, spread_start, 0)

    for q in range(1, teams):
        grad_copy(q).wait()
    g = grad_ref[pl.ds(pl.multiple_of(core * portion, SUB), portion), :]
    for q in range(1, teams):
        g = g + got_grad[q - 1]
    x = own_ref[...].astype(jnp.float32)
    inv = lax.rsqrt(jnp.mean(x * x, axis=-1, keepdims=True) + norm_eps)
    xhat = x * inv
    gx = g * gain_ref[...]
    inner = jnp.mean(gx * xhat, axis=-1, keepdims=True)
    hid_out[...] = (inv * (gx - xhat * inner)).astype(jnp.bfloat16)

    def spread_wait(step, carry):
        spread_copy(step).wait()
        return carry

    lax.fori_loop(1, n, spread_wait, 0)
    for j in range(gain_rows):
        gain_out[:, j * LANES:(j + 1) * LANES] = (
            merged[j // per, pl.ds(j % per, 1), :] / total_rows
        )
    j = gain_rows
    loss_out[...] = merged[j // per, pl.ds(j % per, 1), :] / loss_scale
    for i in range(bias_rows):
        j = gain_rows + 1 + i
        bias_out[:, i * LANES:(i + 1) * LANES] = (
            merged[j // per, pl.ds(j % per, 1), :] / total_rows
        )


def tail_call(grad_all, gathered, hidden, gain, bias_part, loss_part, total_rows, loss_scale):
    n = lax.axis_size("dp")
    teams = lax.axis_size("tensor")
    portion, depth = hidden.shape
    cols = bias_part.shape[1]
    lines = depth // LANES + 1 + cols // LANES
    per = -(-lines // n)
    deep = -(-per // SUB) * SUB
    vmem = pl.BlockSpec(memory_space=pltpu.VMEM)
    dma = pltpu.SemaphoreType.DMA
    return pl.pallas_call(
        functools.partial(tail_kernel, n, teams, per, float(total_rows), float(loss_scale)),
        out_shape=(
            jax.ShapeDtypeStruct((portion, depth), jnp.bfloat16),
            jax.ShapeDtypeStruct((1, depth), jnp.float32),
            jax.ShapeDtypeStruct((1, cols), jnp.float32),
            jax.ShapeDtypeStruct((1, LANES), jnp.float32),
        ),
        in_specs=[vmem] * 6,
        out_specs=(vmem,) * 4,
        scratch_shapes=[
            pltpu.VMEM((teams - 1, portion, depth), jnp.float32),
            pltpu.VMEM((n, deep, LANES), jnp.float32),
            pltpu.VMEM((n - 1, deep, LANES), jnp.float32),
            pltpu.VMEM((deep, LANES), jnp.float32),
            pltpu.VMEM((teams - 1, deep, LANES), jnp.float32),
            pltpu.VMEM((n, deep, LANES), jnp.float32),
            dma((teams - 1,)), dma((teams - 1,)),
            dma((n - 1,)), dma((n - 1,)),
            dma((teams - 1,)), dma((teams - 1,)),
            dma((n - 1,)), dma((n - 1,)),
        ],
        compiler_params=pltpu.CompilerParams(
            collective_id=0, has_side_effects=True, vmem_limit_bytes=VMEM_LIMIT
        ),
        name="tail",
    )(grad_all, gathered, hidden, gain, bias_part, loss_part)


def moved(value, steps):
    count = lax.axis_size("dp")
    if steps % count == 0:
        return value
    return lax.ppermute(value, "dp", [(s, (s - steps) % count) for s in range(count)])


def gather_team(hidden):
    teams = lax.axis_size("tensor")
    core = lax.axis_index("tensor")
    portion = hidden.shape[0]
    pieces = [hidden]
    for q in range(1, teams):
        pieces.append(lax.ppermute(hidden, "tensor", [(s, (s + q) % teams) for s in range(teams)]))
    if teams == 2:
        return jnp.where(
            core == 0,
            jnp.concatenate(pieces, axis=0),
            jnp.concatenate(pieces[::-1], axis=0),
        )
    full = jnp.zeros((portion * teams, hidden.shape[1]), hidden.dtype)
    for q in range(teams):
        at = lax.rem(core - q + teams, teams) * portion
        full = lax.dynamic_update_slice_in_dim(full, pieces[q], at, 0)
    return full


def shards(hidden, doc_ids, teacher, rotation, norm_gain_vector, proj_bias, projection):
    members = lax.axis_size("dp")
    here = lax.axis_index("dp")
    turn = rotation[0] % members
    block_rows = hidden.shape[0] * lax.axis_size("tensor")
    overall_rows = block_rows * members
    total_cols = projection.shape[1] * lax.axis_size("tensor")
    gain = norm_gain_vector.reshape(1, -1)
    bias = proj_bias.reshape(1, -1)

    digit = min(members, MOST_DIRECT)
    unit = 1
    while unit * digit < members:
        branches = [functools.partial(moved, steps=i * unit) for i in range(digit)]
        teacher = lax.switch((turn // unit) % digit, branches, teacher)
        unit = unit * digit

    def last(steps):
        def body(teacher, hidden, doc_ids):
            target = moved(teacher, steps)
            gathered = gather_team(hidden)
            logits = logits_call(gathered, gain, projection, bias)
            row_docs = lax.dynamic_slice_in_dim(doc_ids, here, 1, 0)[0]
            same = jnp.sum((row_docs[:, None] == row_docs[None, :]).astype(jnp.float32), axis=-1)
            weight = (block_rows / (DOCS * same))[:, None]
            return target, gathered, logits, weight

        return body

    count = -(-members // unit)
    target, gathered, logits, weight = lax.switch(
        turn // unit, [last(i * unit) for i in range(count)], teacher, hidden, doc_ids
    )
    grad_all, bias_part, loss_part = grad_call(logits, target, weight, projection)
    hid, gain_mean, bias_mean, loss = tail_call(
        grad_all, gathered, hidden, gain, bias_part, loss_part,
        overall_rows, 2.0 * overall_rows * total_cols,
    )
    return hid, gain_mean.reshape(-1), bias_mean.reshape(-1), loss[0, 0]


def solution(mesh):
    return jax.shard_map(
        shards,
        mesh=mesh,
        in_specs=(
            P(("dp", "tensor"), None),
            P(),
            P("dp", "tensor"),
            P(),
            P(),
            P("tensor"),
            P(None, "tensor"),
        ),
        out_specs=(P(("dp", "tensor"), None), P(), P("tensor"), P()),
        check_vma=False,
    )
```

```python
import functools

import jax
import jax.numpy as jnp
from jax import lax
from jax.experimental import pallas as pl
from jax.experimental.pallas import tpu as pltpu
from jax.sharding import PartitionSpec as P

DOCS = 4
norm_eps = 1e-05
LANES = 128
SUB = 8
MESH = pl.DeviceIdType.MESH
VMEM_LIMIT = 56 * 1024 * 1024
MOST_DIRECT = 16


def divisor_tile(width, most):
    units = width // LANES
    best = max(u for u in range(1, units + 1) if units % u == 0 and u * LANES <= most)
    return best * LANES


def block_kernel(
    steps, n, teams, blocks,
    hid_ref, teacher_ref, weight_ref, gain_ref, bias_ref, w_ref,
    hid_out, gain_out, bias_out, loss_out,
    w_all, logits, target, full, xhat, normed, acc, got_grad,
    w_sem, hs, hr, xs, xr, gs, gr,
):
    here = lax.axis_index("dp")
    core = lax.axis_index("tensor")
    portion, depth = hid_ref.shape
    chunks, rows, tile = logits.shape
    source = lax.rem(here + steps, n)
    taker = lax.rem(here + n - steps, n)

    def w_copy(i):
        at = pl.ds(pl.multiple_of(i * tile, LANES), tile)
        return pltpu.make_async_copy(w_ref.at[:, at], w_all.at[i], w_sem.at[i])

    def w_start(i, carry):
        w_copy(i).start()
        return carry

    def target_copy(i):
        at = pl.ds(pl.multiple_of(i * tile, LANES), tile)
        if steps == 0:
            return pltpu.make_async_copy(teacher_ref.at[:, at], target.at[i], xr.at[i])
        return pltpu.make_async_remote_copy(
            src_ref=teacher_ref.at[:, at],
            dst_ref=target.at[i],
            send_sem=xs.at[i],
            recv_sem=xr.at[i],
            device_id=(taker, core),
            device_id_type=MESH,
        )

    def target_start(i, carry):
        target_copy(i).start()
        return carry

    def hidden_copy(q):
        return pltpu.make_async_remote_copy(
            src_ref=hid_ref,
            dst_ref=full.at[core],
            send_sem=hs.at[q - 1],
            recv_sem=hr.at[q - 1],
            device_id=(here, lax.rem(core + q, teams)),
            device_id_type=MESH,
        )

    barrier = pltpu.get_barrier_semaphore()
    if steps:
        pl.semaphore_signal(barrier, inc=1, device_id=(source, core), device_id_type=MESH)
    for q in range(1, teams):
        pl.semaphore_signal(
            barrier, inc=1, device_id=(here, lax.rem(core + q, teams)), device_id_type=MESH
        )
    w_copy(0).start()
    pl.semaphore_wait(barrier, teams - 1 + (1 if steps else 0))
    for q in range(1, teams):
        hidden_copy(q).start()
    lax.fori_loop(0, chunks, target_start, 0)
    lax.fori_loop(1, chunks, w_start, 0)

    full[core] = hid_ref[...]
    acc[...] = jnp.zeros_like(acc)
    loss_out[...] = jnp.zeros_like(loss_out)
    for q in range(1, teams):
        hidden_copy(q).wait()
    for j in range(teams):
        x = full[j].astype(jnp.float32)
        inv = lax.rsqrt(jnp.mean(x * x, axis=-1, keepdims=True) + norm_eps)
        xhat[j * portion:(j + 1) * portion, :] = x * inv
    normed[...] = (xhat[...] * gain_ref[...]).astype(jnp.bfloat16)

    def forward(i, carry):
        w_copy(i).wait()
        logits[i] = (
            jnp.dot(normed[...], w_all[i], preferred_element_type=jnp.float32) + bias_ref[i]
        )
        return carry

    lax.fori_loop(0, chunks, forward, 0)

    def backward(i, carry):
        target_copy(i).wait()
        error = logits[i] - target[i].astype(jnp.float32)
        weighted = weight_ref[...] * error
        loss_out[...] += jnp.sum(weighted * error, axis=0, keepdims=True)
        rounded = weighted.astype(jnp.bfloat16)
        bias_out[i] = jnp.sum(rounded.astype(jnp.float32), axis=0, keepdims=True)
        for at in range(0, depth, blocks):
            acc[:, at:at + blocks] += lax.dot_general(
                rounded, w_all[i, at:at + blocks, :], (((1,), (1,)), ((), ())),
                preferred_element_type=jnp.float32,
            )
        return carry

    lax.fori_loop(0, chunks, backward, 0)

    def grad_copy(q):
        peer = lax.rem(core + q, teams)
        return pltpu.make_async_remote_copy(
            src_ref=acc.at[pl.ds(pl.multiple_of(peer * portion, SUB), portion), :],
            dst_ref=got_grad.at[q - 1],
            send_sem=gs.at[q - 1],
            recv_sem=gr.at[q - 1],
            device_id=(here, peer),
            device_id_type=MESH,
        )

    for q in range(1, teams):
        grad_copy(q).start()
    gain_out[...] = jnp.sum(acc[...] * xhat[...], axis=0, keepdims=True)
    x = hid_ref[...].astype(jnp.float32)
    inv = lax.rsqrt(jnp.mean(x * x, axis=-1, keepdims=True) + norm_eps)
    own = x * inv
    for q in range(1, teams):
        grad_copy(q).wait()
    g = acc[pl.ds(pl.multiple_of(core * portion, SUB), portion), :]
    for q in range(1, teams):
        g = g + got_grad[q - 1]
    gx = g * gain_ref[...]
    inner = jnp.mean(gx * own, axis=-1, keepdims=True)
    hid_out[...] = (inv * (gx - own * inner)).astype(jnp.bfloat16)


def block_call(steps, mark, hidden, teacher, weight, gain, bias, projection):
    n = lax.axis_size("dp")
    teams = lax.axis_size("tensor")
    portion, depth = hidden.shape
    rows, cols = teacher.shape
    tile = divisor_tile(cols, 512)
    chunks = cols // tile
    vmem = pl.BlockSpec(memory_space=pltpu.VMEM)
    anyspace = pl.BlockSpec(memory_space=pl.ANY)
    dma = pltpu.SemaphoreType.DMA
    return pl.pallas_call(
        functools.partial(block_kernel, steps, n, teams, divisor_tile(depth, 1024)),
        out_shape=(
            jax.ShapeDtypeStruct((portion, depth), jnp.bfloat16),
            jax.ShapeDtypeStruct((1, depth), jnp.float32),
            jax.ShapeDtypeStruct((chunks, 1, tile), jnp.float32),
            jax.ShapeDtypeStruct((1, tile), jnp.float32),
        ),
        in_specs=[vmem, anyspace, vmem, vmem, vmem, anyspace],
        out_specs=(vmem,) * 4,
        scratch_shapes=[
            pltpu.VMEM((chunks, depth, tile), jnp.bfloat16),
            pltpu.VMEM((chunks, rows, tile), jnp.float32),
            pltpu.VMEM((chunks, rows, tile), jnp.bfloat16),
            pltpu.VMEM((teams, portion, depth), jnp.bfloat16),
            pltpu.VMEM((rows, depth), jnp.float32),
            pltpu.VMEM((rows, depth), jnp.bfloat16),
            pltpu.VMEM((rows, depth), jnp.float32),
            pltpu.VMEM((teams - 1, portion, depth), jnp.float32),
            dma((chunks,)),
            dma((teams - 1,)), dma((teams - 1,)),
            dma((chunks,)), dma((chunks,)),
            dma((teams - 1,)), dma((teams - 1,)),
        ],
        cost_estimate=pl.CostEstimate(
            flops=4 * rows * depth * cols, bytes_accessed=2 * depth * cols, transcendentals=0
        ),
        compiler_params=pltpu.CompilerParams(
            collective_id=mark, has_side_effects=True, vmem_limit_bytes=VMEM_LIMIT
        ),
        name="block",
    )(hidden, teacher, weight, gain, bias.reshape(chunks, 1, tile), projection)


def tail_kernel(
    n, teams, per, total_rows, loss_scale,
    gain_ref, bias_ref, loss_ref,
    gain_out, bias_out, loss_out,
    own_vec, got_vec, red, got_red, merged,
    ss, sr, ts, tr, bs, br,
):
    here = lax.axis_index("dp")
    core = lax.axis_index("tensor")
    depth = gain_ref.shape[1]
    chunks, _, tile = bias_ref.shape
    cols = chunks * tile
    gain_rows = depth // LANES
    bias_rows = cols // LANES

    barrier = pltpu.get_barrier_semaphore()

    def greet(step, carry):
        pl.semaphore_signal(
            barrier, inc=1, device_id=(lax.rem(here + step, n), core), device_id_type=MESH
        )
        return carry

    lax.fori_loop(1, n, greet, 0)
    for q in range(1, teams):
        pl.semaphore_signal(
            barrier, inc=1, device_id=(here, lax.rem(core + q, teams)), device_id_type=MESH
        )
    pl.semaphore_wait(barrier, n - 1 + teams - 1)

    loss_part = jnp.sum(loss_ref[...], axis=-1, keepdims=True)

    own_vec[...] = jnp.zeros_like(own_vec)
    for j in range(gain_rows):
        own_vec[j // per, pl.ds(j % per, 1), :] = gain_ref[:, j * LANES:(j + 1) * LANES]
    j = gain_rows
    own_vec[j // per, pl.ds(j % per, 1), :] = jnp.broadcast_to(loss_part, (1, LANES))
    for i in range(bias_rows):
        j = gain_rows + 1 + i
        at = i * LANES % tile
        own_vec[j // per, pl.ds(j % per, 1), :] = bias_ref[i * LANES // tile, :, at:at + LANES]

    def scatter_copy(step):
        peer = lax.rem(here + step, n)
        return pltpu.make_async_remote_copy(
            src_ref=own_vec.at[peer],
            dst_ref=got_vec.at[step - 1],
            send_sem=ss.at[step - 1],
            recv_sem=sr.at[step - 1],
            device_id=(peer, core),
            device_id_type=MESH,
        )

    def scatter_start(step, carry):
        scatter_copy(step).start()
        return carry

    lax.fori_loop(1, n, scatter_start, 0)

    def scatter_wait(step, total):
        scatter_copy(step).wait()
        return total + got_vec[step - 1]

    red[...] = lax.fori_loop(1, n, scatter_wait, own_vec[here])

    def team_copy(q):
        peer = lax.rem(core + q, teams)
        return pltpu.make_async_remote_copy(
            src_ref=red,
            dst_ref=got_red.at[q - 1],
            send_sem=ts.at[q - 1],
            recv_sem=tr.at[q - 1],
            device_id=(here, peer),
            device_id_type=MESH,
        )

    for q in range(1, teams):
        team_copy(q).start()
    for q in range(1, teams):
        team_copy(q).wait()
    others = jnp.zeros(red.shape, jnp.float32)
    for q in range(1, teams):
        others = others + got_red[q - 1]
    row_at = here * per + lax.broadcasted_iota(jnp.int32, red.shape, 0)
    merged[here] = red[...] + jnp.where(row_at <= gain_rows, others, 0.0)

    def spread_copy(step):
        peer = lax.rem(here + step, n)
        return pltpu.make_async_remote_copy(
            src_ref=merged.at[here],
            dst_ref=merged.at[here],
            send_sem=bs.at[step - 1],
            recv_sem=br.at[step - 1],
            device_id=(peer, core),
            device_id_type=MESH,
        )

    def spread_start(step, carry):
        spread_copy(step).start()
        return carry

    lax.fori_loop(1, n, spread_start, 0)

    def spread_wait(step, carry):
        spread_copy(step).wait()
        return carry

    lax.fori_loop(1, n, spread_wait, 0)
    for j in range(gain_rows):
        gain_out[:, j * LANES:(j + 1) * LANES] = (
            merged[j // per, pl.ds(j % per, 1), :] / total_rows
        )
    j = gain_rows
    loss_out[...] = merged[j // per, pl.ds(j % per, 1), :] / loss_scale
    for i in range(bias_rows):
        j = gain_rows + 1 + i
        bias_out[:, i * LANES:(i + 1) * LANES] = (
            merged[j // per, pl.ds(j % per, 1), :] / total_rows
        )


def tail_call(gain_part, bias_part, loss_part, total_rows, loss_scale):
    n = lax.axis_size("dp")
    teams = lax.axis_size("tensor")
    depth = gain_part.shape[1]
    cols = bias_part.size
    lines = depth // LANES + 1 + cols // LANES
    per = -(-lines // n)
    deep = -(-per // SUB) * SUB
    vmem = pl.BlockSpec(memory_space=pltpu.VMEM)
    dma = pltpu.SemaphoreType.DMA
    return pl.pallas_call(
        functools.partial(tail_kernel, n, teams, per, float(total_rows), float(loss_scale)),
        out_shape=(
            jax.ShapeDtypeStruct((1, depth), jnp.float32),
            jax.ShapeDtypeStruct((1, cols), jnp.float32),
            jax.ShapeDtypeStruct((1, LANES), jnp.float32),
        ),
        in_specs=[vmem] * 3,
        out_specs=(vmem,) * 3,
        scratch_shapes=[
            pltpu.VMEM((n, deep, LANES), jnp.float32),
            pltpu.VMEM((n - 1, deep, LANES), jnp.float32),
            pltpu.VMEM((deep, LANES), jnp.float32),
            pltpu.VMEM((teams - 1, deep, LANES), jnp.float32),
            pltpu.VMEM((n, deep, LANES), jnp.float32),
            dma((n - 1,)), dma((n - 1,)),
            dma((teams - 1,)), dma((teams - 1,)),
            dma((n - 1,)), dma((n - 1,)),
        ],
        compiler_params=pltpu.CompilerParams(
            collective_id=0, has_side_effects=True, vmem_limit_bytes=VMEM_LIMIT
        ),
        name="tail",
    )(gain_part, bias_part, loss_part)


def moved(value, steps):
    count = lax.axis_size("dp")
    if steps % count == 0:
        return value
    return lax.ppermute(value, "dp", [(s, (s - steps) % count) for s in range(count)])


def shards(hidden, doc_ids, teacher, rotation, norm_gain_vector, proj_bias, projection):
    members = lax.axis_size("dp")
    here = lax.axis_index("dp")
    turn = rotation[0] % members
    block_rows = hidden.shape[0] * lax.axis_size("tensor")
    overall_rows = block_rows * members
    total_cols = projection.shape[1] * lax.axis_size("tensor")
    gain = norm_gain_vector.reshape(1, -1)
    bias = proj_bias.reshape(1, -1)

    digit = min(members, MOST_DIRECT)
    unit = 1
    while unit * digit < members:
        branches = [functools.partial(moved, steps=i * unit) for i in range(digit)]
        teacher = lax.switch((turn // unit) % digit, branches, teacher)
        unit = unit * digit

    row_docs = lax.dynamic_slice_in_dim(doc_ids, here, 1, 0)[0]
    same = jnp.sum((row_docs[:, None] == row_docs[None, :]).astype(jnp.float32), axis=-1)
    weight = (block_rows / (DOCS * same))[:, None]
    count = -(-members // unit)
    branches = [functools.partial(block_call, i * unit, 1 + i) for i in range(count)]
    hid, gain_part, bias_part, loss_part = lax.switch(
        turn // unit, branches, hidden, teacher, weight, gain, bias, projection
    )
    gain_mean, bias_mean, loss = tail_call(
        gain_part, bias_part, loss_part, overall_rows, 2.0 * overall_rows * total_cols
    )
    return hid, gain_mean.reshape(-1), bias_mean.reshape(-1), loss[0, 0]


def solution(mesh):
    return jax.shard_map(
        shards,
        mesh=mesh,
        in_specs=(
            P(("dp", "tensor"), None),
            P(),
            P("dp", "tensor"),
            P(),
            P(),
            P("tensor"),
            P(None, "tensor"),
        ),
        out_specs=(P(("dp", "tensor"), None), P(), P("tensor"), P()),
        check_vma=False,
    )
```

```python
import functools

import jax
import jax.numpy as jnp
from jax import lax
from jax.experimental import pallas as pl
from jax.experimental.pallas import tpu as pltpu
from jax.sharding import PartitionSpec as P

DOCS = 4
norm_eps = 1e-05
LANES = 128
SUB = 8
MESH = pl.DeviceIdType.MESH
VMEM_LIMIT = 56 * 1024 * 1024
MOST_DIRECT = 16


def divisor_tile(width, most):
    units = width // LANES
    best = max(u for u in range(1, units + 1) if units % u == 0 and u * LANES <= most)
    return best * LANES


def block_kernel(
    steps, n, teams, block, deep,
    hid_ref, teacher_ref, weight_ref, gain_ref, bias_ref, w_ref,
    hid_out, vec_out,
    w_all, logits, target, full, xhat, normed, acc, got_grad, inverse, rounded,
    w_sem, hs, hr, xs, xr, gs, gr,
):
    here = lax.axis_index("dp")
    core = lax.axis_index("tensor")
    portion, depth = hid_ref.shape
    chunks, rows, tile = logits.shape
    source = lax.rem(here + steps, n)
    taker = lax.rem(here + n - steps, n)

    def w_copy(i):
        at = pl.ds(pl.multiple_of(i * tile, LANES), tile)
        return pltpu.make_async_copy(w_ref.at[:, at], w_all.at[i], w_sem.at[i])

    def w_start(i, carry):
        w_copy(i).start()
        return carry

    def target_copy(i):
        at = pl.ds(pl.multiple_of(i * tile, LANES), tile)
        if steps == 0:
            return pltpu.make_async_copy(teacher_ref.at[:, at], target.at[i], xr.at[i])
        return pltpu.make_async_remote_copy(
            src_ref=teacher_ref.at[:, at],
            dst_ref=target.at[i],
            send_sem=xs.at[i],
            recv_sem=xr.at[i],
            device_id=(taker, core),
            device_id_type=MESH,
        )

    def target_start(i, carry):
        target_copy(i).start()
        return carry

    def hidden_copy(q):
        return pltpu.make_async_remote_copy(
            src_ref=hid_ref,
            dst_ref=full.at[core],
            send_sem=hs.at[q - 1],
            recv_sem=hr.at[q - 1],
            device_id=(here, lax.rem(core + q, teams)),
            device_id_type=MESH,
        )

    barrier = pltpu.get_barrier_semaphore()
    if steps:
        pl.semaphore_signal(barrier, inc=1, device_id=(source, core), device_id_type=MESH)
    for q in range(1, teams):
        pl.semaphore_signal(
            barrier, inc=1, device_id=(here, lax.rem(core + q, teams)), device_id_type=MESH
        )
    w_copy(0).start()
    pl.semaphore_wait(barrier, teams - 1 + (1 if steps else 0))
    for q in range(1, teams):
        hidden_copy(q).start()
    lax.fori_loop(0, chunks, target_start, 0)
    lax.fori_loop(1, chunks, w_start, 0)

    full[core] = hid_ref[...]

    def spans(c):
        return pl.ds(pl.multiple_of(c * block, LANES), block)

    pieces = depth // block
    for q in range(1, teams):
        hidden_copy(q).wait()

    def squares(c, totals):
        out = []
        for j in range(teams):
            x = full[j, :, spans(c)].astype(jnp.float32)
            out.append(totals[j] + jnp.sum(x * x, axis=-1, keepdims=True))
        return tuple(out)

    totals = lax.fori_loop(
        0, pieces, squares, tuple(jnp.zeros((portion, 1), jnp.float32) for _ in range(teams))
    )
    for j in range(teams):
        inverse[j] = jnp.broadcast_to(
            lax.rsqrt(totals[j] / depth + norm_eps), (portion, LANES)
        )

    def normalise(c, carry):
        for j in range(teams):
            x = full[j, :, spans(c)].astype(jnp.float32)
            xhat[j * portion:(j + 1) * portion, spans(c)] = x * inverse[j, :, 0:1]
        normed[:, spans(c)] = (xhat[:, spans(c)] * gain_ref[:, spans(c)]).astype(jnp.bfloat16)
        acc[:, spans(c)] = jnp.zeros((rows, block), jnp.float32)
        return carry

    lax.fori_loop(0, pieces, normalise, 0)

    lines = tile // LANES
    gain_rows = depth // LANES
    bias_rows = chunks * lines
    vec_out[...] = jnp.zeros_like(vec_out)

    def forward(i, carry):
        w_copy(i).wait()
        bias = jnp.concatenate([bias_ref[pl.ds(i * lines + k, 1), :] for k in range(lines)], axis=1)
        logits[i] = jnp.broadcast_to(bias, (rows, tile))

        def inner(c, done):
            at = pl.ds(pl.multiple_of(c * deep, LANES), deep)
            logits[i] += jnp.dot(
                normed[:, at], w_all[i, at, :], preferred_element_type=jnp.float32
            )
            return done

        return lax.fori_loop(0, depth // deep, inner, carry)

    lax.fori_loop(0, chunks, forward, 0)

    def backward(i, carry):
        target_copy(i).wait()
        error = logits[i] - target[i].astype(jnp.float32)
        weighted = weight_ref[:, 0:1] * error
        losses = jnp.sum(weighted * error, axis=0, keepdims=True)
        rounded[...] = weighted.astype(jnp.bfloat16)
        sums = jnp.sum(rounded[...].astype(jnp.float32), axis=0, keepdims=True)
        for k in range(lines):
            part = slice(k * LANES, (k + 1) * LANES)
            vec_out[pl.ds(gain_rows + i * lines + k, 1), :] = sums[:, part]
            vec_out[gain_rows + bias_rows:gain_rows + bias_rows + 1, :] += losses[:, part]

        def inner(c, done):
            at = pl.ds(pl.multiple_of(c * deep, LANES), deep)
            acc[:, at] += lax.dot_general(
                rounded[...], w_all[i, at, :], (((1,), (1,)), ((), ())),
                preferred_element_type=jnp.float32,
            )
            return done

        return lax.fori_loop(0, depth // deep, inner, carry)

    lax.fori_loop(0, chunks, backward, 0)

    def grad_copy(q):
        peer = lax.rem(core + q, teams)
        return pltpu.make_async_remote_copy(
            src_ref=acc.at[pl.ds(pl.multiple_of(peer * portion, SUB), portion), :],
            dst_ref=got_grad.at[q - 1],
            send_sem=gs.at[q - 1],
            recv_sem=gr.at[q - 1],
            device_id=(here, peer),
            device_id_type=MESH,
        )

    for q in range(1, teams):
        grad_copy(q).start()

    def gains(c, carry):
        sums = jnp.sum(acc[:, spans(c)] * xhat[:, spans(c)], axis=0, keepdims=True)
        for k in range(block // LANES):
            vec_out[pl.ds(c * (block // LANES) + k, 1), :] = sums[:, k * LANES:(k + 1) * LANES]
        return carry

    lax.fori_loop(0, pieces, gains, 0)
    for q in range(1, teams):
        grad_copy(q).wait()
    mine = pl.ds(pl.multiple_of(core * portion, SUB), portion)

    def scaled(c):
        g = acc[mine, spans(c)]
        for q in range(1, teams):
            g = g + got_grad[q - 1, :, spans(c)]
        return g * gain_ref[:, spans(c)]

    def inners(c, total):
        return total + jnp.sum(scaled(c) * xhat[mine, spans(c)], axis=-1, keepdims=True)

    inner_mean = lax.fori_loop(0, pieces, inners, jnp.zeros((portion, 1), jnp.float32)) / depth
    inv = inverse[core][:, 0:1]

    def finish(c, carry):
        own = xhat[mine, spans(c)]
        hid_out[:, spans(c)] = (inv * (scaled(c) - own * inner_mean)).astype(jnp.bfloat16)
        return carry

    lax.fori_loop(0, pieces, finish, 0)


def slice_rows(lines, n):
    per = SUB * -(-lines // (SUB * n))
    return per, -(-lines // per)


def block_call(steps, mark, hidden, teacher, weight, gain, bias, projection):
    n = lax.axis_size("dp")
    teams = lax.axis_size("tensor")
    portion, depth = hidden.shape
    rows, cols = teacher.shape
    tile = divisor_tile(cols, 512)
    chunks = cols // tile
    per, owners = slice_rows((depth + cols) // LANES + 1, n)
    vmem = pl.BlockSpec(memory_space=pltpu.VMEM)
    anyspace = pl.BlockSpec(memory_space=pl.ANY)
    dma = pltpu.SemaphoreType.DMA
    return pl.pallas_call(
        functools.partial(
            block_kernel, steps, n, teams, divisor_tile(depth, 256), divisor_tile(depth, 1024)
        ),
        out_shape=(
            jax.ShapeDtypeStruct((portion, depth), jnp.bfloat16),
            jax.ShapeDtypeStruct((per * owners, LANES), jnp.float32),
        ),
        in_specs=[vmem, anyspace, vmem, vmem, vmem, anyspace],
        out_specs=(vmem,) * 2,
        scratch_shapes=[
            pltpu.VMEM((chunks, depth, tile), jnp.bfloat16),
            pltpu.VMEM((chunks, rows, tile), jnp.float32),
            pltpu.VMEM((chunks, rows, tile), jnp.bfloat16),
            pltpu.VMEM((teams, portion, depth), jnp.bfloat16),
            pltpu.VMEM((rows, depth), jnp.float32),
            pltpu.VMEM((rows, depth), jnp.bfloat16),
            pltpu.VMEM((rows, depth), jnp.float32),
            pltpu.VMEM((teams - 1, portion, depth), jnp.float32),
            pltpu.VMEM((teams, portion, LANES), jnp.float32),
            pltpu.VMEM((rows, tile), jnp.bfloat16),
            dma((chunks,)),
            dma((teams - 1,)), dma((teams - 1,)),
            dma((chunks,)), dma((chunks,)),
            dma((teams - 1,)), dma((teams - 1,)),
        ],
        cost_estimate=pl.CostEstimate(
            flops=4 * rows * depth * cols, bytes_accessed=2 * depth * cols, transcendentals=0
        ),
        compiler_params=pltpu.CompilerParams(
            collective_id=mark, has_side_effects=True, vmem_limit_bytes=VMEM_LIMIT
        ),
        name="block",
    )(hidden, teacher, weight, gain, bias, projection)


def tail_kernel(
    n, teams, per, owners, gain_rows, bias_rows, total_rows, loss_scale,
    vec_ref,
    gain_out, bias_out, loss_out,
    got_vec, red, got_red, merged,
    ss, sr, ts, tr, bs, br,
):
    here = lax.axis_index("dp")
    core = lax.axis_index("tensor")

    barrier = pltpu.get_barrier_semaphore()

    def greet(step, carry):
        pl.semaphore_signal(
            barrier, inc=1, device_id=(lax.rem(here + step, n), core), device_id_type=MESH
        )
        return carry

    lax.fori_loop(1, n, greet, 0)
    for q in range(1, teams):
        pl.semaphore_signal(
            barrier, inc=1, device_id=(here, lax.rem(core + q, teams)), device_id_type=MESH
        )
    pl.semaphore_wait(barrier, n - 1 + teams - 1)

    def scatter_copy(step):
        peer = lax.rem(here + step, n)
        held = lax.rem(peer, owners)
        return pltpu.make_async_remote_copy(
            src_ref=vec_ref.at[pl.ds(pl.multiple_of(held * per, SUB), per), :],
            dst_ref=got_vec.at[step - 1],
            send_sem=ss.at[step - 1],
            recv_sem=sr.at[step - 1],
            device_id=(peer, core),
            device_id_type=MESH,
        )

    def spread_copy(step):
        peer = lax.rem(here + step, n)
        spot = merged.at[lax.rem(here, owners)]
        return pltpu.make_async_remote_copy(
            src_ref=spot,
            dst_ref=spot,
            send_sem=bs.at[step - 1],
            recv_sem=br.at[step - 1],
            device_id=(peer, core),
            device_id_type=MESH,
        )

    def scatter_start(step, carry):
        @pl.when(lax.rem(here + step, n) < owners)
        def _():
            scatter_copy(step).start()

        return carry

    lax.fori_loop(1, n, scatter_start, 0)

    def team_copy(q):
        peer = lax.rem(core + q, teams)
        return pltpu.make_async_remote_copy(
            src_ref=red,
            dst_ref=got_red.at[q - 1],
            send_sem=ts.at[q - 1],
            recv_sem=tr.at[q - 1],
            device_id=(here, peer),
            device_id_type=MESH,
        )

    @pl.when(here < owners)
    def _():
        def scatter_wait(step, total):
            scatter_copy(step).wait_recv()
            return total + got_vec[step - 1]

        red[...] = lax.fori_loop(
            1, n, scatter_wait, vec_ref[pl.ds(pl.multiple_of(here * per, SUB), per), :]
        )
        for q in range(1, teams):
            team_copy(q).start()
        for q in range(1, teams):
            team_copy(q).wait()
        others = jnp.zeros(red.shape, jnp.float32)
        for q in range(1, teams):
            others = others + got_red[q - 1]
        row_at = here * per + lax.broadcasted_iota(jnp.int32, red.shape, 0)
        shared = (row_at < gain_rows) | (row_at >= gain_rows + bias_rows)
        merged[here] = red[...] + jnp.where(shared, others, 0.0)

        def spread_start(step, carry):
            spread_copy(step).start()
            return carry

        lax.fori_loop(1, n, spread_start, 0)

    def settle(step, carry):
        @pl.when(lax.rem(here + step, n) < owners)
        def _():
            scatter_copy(step).wait_send()

        @pl.when(lax.rem(here + n - step, n) < owners)
        def _():
            spread_copy(step).wait_recv()

        @pl.when(here < owners)
        def _():
            spread_copy(step).wait_send()

        return carry

    lax.fori_loop(1, n, settle, 0)
    whole = merged[...].reshape(owners * per, LANES)
    gain_out[...] = whole[:gain_rows] / total_rows
    bias_out[...] = whole[gain_rows:gain_rows + bias_rows] / total_rows
    loss = whole[gain_rows + bias_rows:gain_rows + bias_rows + 1]
    loss_out[...] = jnp.sum(loss, axis=-1, keepdims=True) / loss_scale


def tail_call(vec, gain_rows, bias_rows, total_rows, loss_scale):
    n = lax.axis_size("dp")
    teams = lax.axis_size("tensor")
    per, owners = slice_rows(gain_rows + bias_rows + 1, n)
    vmem = pl.BlockSpec(memory_space=pltpu.VMEM)
    dma = pltpu.SemaphoreType.DMA
    return pl.pallas_call(
        functools.partial(
            tail_kernel, n, teams, per, owners, gain_rows, bias_rows,
            float(total_rows), float(loss_scale),
        ),
        out_shape=(
            jax.ShapeDtypeStruct((gain_rows, LANES), jnp.float32),
            jax.ShapeDtypeStruct((bias_rows, LANES), jnp.float32),
            jax.ShapeDtypeStruct((1, 1), jnp.float32),
        ),
        in_specs=[vmem],
        out_specs=(vmem,) * 3,
        scratch_shapes=[
            pltpu.VMEM((n - 1, per, LANES), jnp.float32),
            pltpu.VMEM((per, LANES), jnp.float32),
            pltpu.VMEM((teams - 1, per, LANES), jnp.float32),
            pltpu.VMEM((owners, per, LANES), jnp.float32),
            dma((n - 1,)), dma((n - 1,)),
            dma((teams - 1,)), dma((teams - 1,)),
            dma((n - 1,)), dma((n - 1,)),
        ],
        compiler_params=pltpu.CompilerParams(
            collective_id=0, has_side_effects=True, vmem_limit_bytes=VMEM_LIMIT
        ),
        name="tail",
    )(vec)


def moved(value, steps):
    count = lax.axis_size("dp")
    if steps % count == 0:
        return value
    return lax.ppermute(value, "dp", [(s, (s - steps) % count) for s in range(count)])


def shards(hidden, doc_ids, teacher, rotation, norm_gain_vector, proj_bias, projection):
    members = lax.axis_size("dp")
    here = lax.axis_index("dp")
    turn = rotation[0] % members
    block_rows = hidden.shape[0] * lax.axis_size("tensor")
    overall_rows = block_rows * members
    total_cols = projection.shape[1] * lax.axis_size("tensor")
    gain = norm_gain_vector.reshape(1, -1)
    bias = proj_bias.reshape(-1, LANES)

    digit = min(members, MOST_DIRECT)
    unit = 1
    while unit * digit < members:
        branches = [functools.partial(moved, steps=i * unit) for i in range(digit)]
        teacher = lax.switch((turn // unit) % digit, branches, teacher)
        unit = unit * digit

    row_docs = lax.dynamic_slice_in_dim(doc_ids, here, 1, 0)[0]
    same = jnp.sum((row_docs[:, None] == row_docs[None, :]).astype(jnp.float32), axis=-1)
    weight = jnp.broadcast_to((block_rows / (DOCS * same))[:, None], (block_rows, LANES))
    count = -(-members // unit)
    branches = [functools.partial(block_call, i * unit, 1 + i) for i in range(count)]
    hid, vec = lax.switch(
        turn // unit, branches, hidden, teacher, weight, gain, bias, projection
    )
    gain_mean, bias_mean, loss = tail_call(
        vec, gain.size // LANES, bias.size // LANES, overall_rows, 2.0 * overall_rows * total_cols
    )
    return hid, gain_mean.reshape(-1), bias_mean.reshape(-1), loss[0, 0]


def solution(mesh):
    return jax.shard_map(
        shards,
        mesh=mesh,
        in_specs=(
            P(("dp", "tensor"), None),
            P(),
            P("dp", "tensor"),
            P(),
            P(),
            P("tensor"),
            P(None, "tensor"),
        ),
        out_specs=(P(("dp", "tensor"), None), P(), P("tensor"), P()),
        check_vma=False,
    )
```

```python
import functools

import jax
import jax.numpy as jnp
from jax import lax
from jax.experimental import pallas as pl
from jax.experimental.pallas import tpu as pltpu
from jax.sharding import PartitionSpec as P

DOCS = 4
norm_eps = 1e-05
LANES = 128
SUB = 8
MESH = pl.DeviceIdType.MESH
VMEM_LIMIT = 56 * 1024 * 1024
MOST_DIRECT = 16


def divisor_tile(width, most):
    units = width // LANES
    best = max(u for u in range(1, units + 1) if units % u == 0 and u * LANES <= most)
    return best * LANES


def block_kernel(
    steps, n, teams, block, deep,
    hid_ref, teacher_ref, weight_ref, gain_ref, bias_ref, w_ref,
    hid_out, vec_out,
    w_all, logits, target, full, xhat, normed, acc, got_grad, inverse, rounded, got_vec,
    w_sem, hs, hr, xs, xr, gs, gr, vs, vr,
):
    here = lax.axis_index("dp")
    core = lax.axis_index("tensor")
    portion, depth = hid_ref.shape
    chunks, rows, tile = logits.shape
    source = lax.rem(here + steps, n)
    taker = lax.rem(here + n - steps, n)

    def w_copy(i):
        at = pl.ds(pl.multiple_of(i * tile, LANES), tile)
        return pltpu.make_async_copy(w_ref.at[:, at], w_all.at[i], w_sem.at[i])

    def w_start(i, carry):
        w_copy(i).start()
        return carry

    def target_copy(i):
        at = pl.ds(pl.multiple_of(i * tile, LANES), tile)
        if steps == 0:
            return pltpu.make_async_copy(teacher_ref.at[:, at], target.at[i], xr.at[i])
        return pltpu.make_async_remote_copy(
            src_ref=teacher_ref.at[:, at],
            dst_ref=target.at[i],
            send_sem=xs.at[i],
            recv_sem=xr.at[i],
            device_id=(taker, core),
            device_id_type=MESH,
        )

    def target_start(i, carry):
        target_copy(i).start()
        return carry

    def hidden_copy(q):
        return pltpu.make_async_remote_copy(
            src_ref=hid_ref,
            dst_ref=full.at[core],
            send_sem=hs.at[q - 1],
            recv_sem=hr.at[q - 1],
            device_id=(here, lax.rem(core + q, teams)),
            device_id_type=MESH,
        )

    barrier = pltpu.get_barrier_semaphore()
    if steps:
        pl.semaphore_signal(barrier, inc=1, device_id=(source, core), device_id_type=MESH)
    for q in range(1, teams):
        pl.semaphore_signal(
            barrier, inc=1, device_id=(here, lax.rem(core + q, teams)), device_id_type=MESH
        )
    w_copy(0).start()
    pl.semaphore_wait(barrier, teams - 1 + (1 if steps else 0))
    for q in range(1, teams):
        hidden_copy(q).start()
    lax.fori_loop(0, chunks, target_start, 0)
    lax.fori_loop(1, chunks, w_start, 0)

    full[core] = hid_ref[...]

    def spans(c):
        return pl.ds(pl.multiple_of(c * block, LANES), block)

    pieces = depth // block
    for q in range(1, teams):
        hidden_copy(q).wait()

    def squares(c, totals):
        out = []
        for j in range(teams):
            x = full[j, :, spans(c)].astype(jnp.float32)
            out.append(totals[j] + jnp.sum(x * x, axis=-1, keepdims=True))
        return tuple(out)

    totals = lax.fori_loop(
        0, pieces, squares, tuple(jnp.zeros((portion, 1), jnp.float32) for _ in range(teams))
    )
    for j in range(teams):
        inverse[j] = jnp.broadcast_to(
            lax.rsqrt(totals[j] / depth + norm_eps), (portion, LANES)
        )

    def normalise(c, carry):
        for j in range(teams):
            x = full[j, :, spans(c)].astype(jnp.float32)
            xhat[j * portion:(j + 1) * portion, spans(c)] = x * inverse[j, :, 0:1]
        normed[:, spans(c)] = (xhat[:, spans(c)] * gain_ref[:, spans(c)]).astype(jnp.bfloat16)
        acc[:, spans(c)] = jnp.zeros((rows, block), jnp.float32)
        return carry

    lax.fori_loop(0, pieces, normalise, 0)

    lines = tile // LANES
    gain_rows = depth // LANES
    bias_rows = chunks * lines
    vec_out[...] = jnp.zeros_like(vec_out)

    def forward(i, carry):
        w_copy(i).wait()
        bias = jnp.concatenate([bias_ref[pl.ds(i * lines + k, 1), :] for k in range(lines)], axis=1)
        logits[i] = jnp.broadcast_to(bias, (rows, tile))

        def inner(c, done):
            at = pl.ds(pl.multiple_of(c * deep, LANES), deep)
            logits[i] += jnp.dot(
                normed[:, at], w_all[i, at, :], preferred_element_type=jnp.float32
            )
            return done

        return lax.fori_loop(0, depth // deep, inner, carry)

    lax.fori_loop(0, chunks, forward, 0)

    def backward(i, carry):
        target_copy(i).wait()
        error = logits[i] - target[i].astype(jnp.float32)
        weighted = weight_ref[:, 0:1] * error
        losses = jnp.sum(weighted * error, axis=0, keepdims=True)
        rounded[...] = weighted.astype(jnp.bfloat16)
        sums = jnp.sum(rounded[...].astype(jnp.float32), axis=0, keepdims=True)
        for k in range(lines):
            part = slice(k * LANES, (k + 1) * LANES)
            vec_out[pl.ds(gain_rows + i * lines + k, 1), :] = sums[:, part]
            vec_out[gain_rows + bias_rows:gain_rows + bias_rows + 1, :] += losses[:, part]

        def inner(c, done):
            at = pl.ds(pl.multiple_of(c * deep, LANES), deep)
            acc[:, at] += lax.dot_general(
                rounded[...], w_all[i, at, :], (((1,), (1,)), ((), ())),
                preferred_element_type=jnp.float32,
            )
            return done

        return lax.fori_loop(0, depth // deep, inner, carry)

    lax.fori_loop(0, chunks, backward, 0)

    def grad_copy(q):
        peer = lax.rem(core + q, teams)
        return pltpu.make_async_remote_copy(
            src_ref=acc.at[pl.ds(pl.multiple_of(peer * portion, SUB), portion), :],
            dst_ref=got_grad.at[q - 1],
            send_sem=gs.at[q - 1],
            recv_sem=gr.at[q - 1],
            device_id=(here, peer),
            device_id_type=MESH,
        )

    for q in range(1, teams):
        grad_copy(q).start()

    def gains(c, carry):
        sums = jnp.sum(acc[:, spans(c)] * xhat[:, spans(c)], axis=0, keepdims=True)
        for k in range(block // LANES):
            vec_out[pl.ds(c * (block // LANES) + k, 1), :] = sums[:, k * LANES:(k + 1) * LANES]
        return carry

    lax.fori_loop(0, pieces, gains, 0)

    def vec_copy(q):
        return pltpu.make_async_remote_copy(
            src_ref=vec_out,
            dst_ref=got_vec.at[q - 1],
            send_sem=vs.at[q - 1],
            recv_sem=vr.at[q - 1],
            device_id=(here, lax.rem(core + q, teams)),
            device_id_type=MESH,
        )

    for q in range(1, teams):
        vec_copy(q).start()
    for q in range(1, teams):
        grad_copy(q).wait()
    mine = pl.ds(pl.multiple_of(core * portion, SUB), portion)

    def scaled(c):
        g = acc[mine, spans(c)]
        for q in range(1, teams):
            g = g + got_grad[q - 1, :, spans(c)]
        return g * gain_ref[:, spans(c)]

    def inners(c, total):
        return total + jnp.sum(scaled(c) * xhat[mine, spans(c)], axis=-1, keepdims=True)

    inner_mean = lax.fori_loop(0, pieces, inners, jnp.zeros((portion, 1), jnp.float32)) / depth
    inv = inverse[core][:, 0:1]

    def finish(c, carry):
        own = xhat[mine, spans(c)]
        hid_out[:, spans(c)] = (inv * (scaled(c) - own * inner_mean)).astype(jnp.bfloat16)
        return carry

    lax.fori_loop(0, pieces, finish, 0)
    for q in range(1, teams):
        vec_copy(q).wait()
    row_at = lax.broadcasted_iota(jnp.int32, vec_out.shape, 0)
    shared = (row_at < gain_rows) | (row_at >= gain_rows + bias_rows)
    for q in range(1, teams):
        vec_out[...] += jnp.where(shared, got_vec[q - 1], 0.0)


def slice_rows(lines, n):
    per = SUB * -(-lines // (SUB * n))
    return per, -(-lines // per)


def block_call(steps, mark, hidden, teacher, weight, gain, bias, projection):
    n = lax.axis_size("dp")
    teams = lax.axis_size("tensor")
    portion, depth = hidden.shape
    rows, cols = teacher.shape
    tile = divisor_tile(cols, 512)
    chunks = cols // tile
    per, owners = slice_rows((depth + cols) // LANES + 1, n)
    vmem = pl.BlockSpec(memory_space=pltpu.VMEM)
    anyspace = pl.BlockSpec(memory_space=pl.ANY)
    dma = pltpu.SemaphoreType.DMA
    return pl.pallas_call(
        functools.partial(
            block_kernel, steps, n, teams, divisor_tile(depth, 256), divisor_tile(depth, 2048)
        ),
        out_shape=(
            jax.ShapeDtypeStruct((portion, depth), jnp.bfloat16),
            jax.ShapeDtypeStruct((per * owners, LANES), jnp.float32),
        ),
        in_specs=[vmem, anyspace, vmem, vmem, vmem, anyspace],
        out_specs=(vmem,) * 2,
        scratch_shapes=[
            pltpu.VMEM((chunks, depth, tile), jnp.bfloat16),
            pltpu.VMEM((chunks, rows, tile), jnp.float32),
            pltpu.VMEM((chunks, rows, tile), jnp.bfloat16),
            pltpu.VMEM((teams, portion, depth), jnp.bfloat16),
            pltpu.VMEM((rows, depth), jnp.float32),
            pltpu.VMEM((rows, depth), jnp.bfloat16),
            pltpu.VMEM((rows, depth), jnp.float32),
            pltpu.VMEM((teams - 1, portion, depth), jnp.float32),
            pltpu.VMEM((teams, portion, LANES), jnp.float32),
            pltpu.VMEM((rows, tile), jnp.bfloat16),
            pltpu.VMEM((teams - 1, per * owners, LANES), jnp.float32),
            dma((chunks,)),
            dma((teams - 1,)), dma((teams - 1,)),
            dma((chunks,)), dma((chunks,)),
            dma((teams - 1,)), dma((teams - 1,)),
            dma((teams - 1,)), dma((teams - 1,)),
        ],
        cost_estimate=pl.CostEstimate(
            flops=4 * rows * depth * cols, bytes_accessed=2 * depth * cols, transcendentals=0
        ),
        compiler_params=pltpu.CompilerParams(
            collective_id=mark, has_side_effects=True, vmem_limit_bytes=VMEM_LIMIT
        ),
        name="block",
    )(hidden, teacher, weight, gain, bias, projection)


def tail_kernel(
    n, per, owners, gain_rows, bias_rows,
    vec_ref,
    gain_out, bias_out, loss_out,
    got_vec, merged,
    ss, sr, bs, br,
):
    here = lax.axis_index("dp")
    core = lax.axis_index("tensor")

    barrier = pltpu.get_barrier_semaphore()

    def greet(step, carry):
        pl.semaphore_signal(
            barrier, inc=1, device_id=(lax.rem(here + step, n), core), device_id_type=MESH
        )
        return carry

    lax.fori_loop(1, n, greet, 0)
    pl.semaphore_wait(barrier, n - 1)

    def scatter_copy(step):
        peer = lax.rem(here + step, n)
        held = lax.rem(peer, owners)
        return pltpu.make_async_remote_copy(
            src_ref=vec_ref.at[pl.ds(pl.multiple_of(held * per, SUB), per), :],
            dst_ref=got_vec.at[step - 1],
            send_sem=ss.at[step - 1],
            recv_sem=sr.at[step - 1],
            device_id=(peer, core),
            device_id_type=MESH,
        )

    def spread_copy(step):
        peer = lax.rem(here + step, n)
        spot = merged.at[lax.rem(here, owners)]
        return pltpu.make_async_remote_copy(
            src_ref=spot,
            dst_ref=spot,
            send_sem=bs.at[step - 1],
            recv_sem=br.at[step - 1],
            device_id=(peer, core),
            device_id_type=MESH,
        )

    def scatter_start(step, carry):
        @pl.when(lax.rem(here + step, n) < owners)
        def _():
            scatter_copy(step).start()

        return carry

    lax.fori_loop(1, n, scatter_start, 0)

    @pl.when(here < owners)
    def _():
        def scatter_wait(step, total):
            scatter_copy(step).wait_recv()
            return total + got_vec[step - 1]

        merged[here] = lax.fori_loop(
            1, n, scatter_wait, vec_ref[pl.ds(pl.multiple_of(here * per, SUB), per), :]
        )

        def spread_start(step, carry):
            spread_copy(step).start()
            return carry

        lax.fori_loop(1, n, spread_start, 0)

    def settle(step, carry):
        @pl.when(lax.rem(here + step, n) < owners)
        def _():
            scatter_copy(step).wait_send()

        @pl.when(lax.rem(here + n - step, n) < owners)
        def _():
            spread_copy(step).wait_recv()

        @pl.when(here < owners)
        def _():
            spread_copy(step).wait_send()

        return carry

    lax.fori_loop(1, n, settle, 0)
    whole = merged[...].reshape(owners * per, LANES)
    gain_out[...] = whole[:gain_rows]
    bias_out[...] = whole[gain_rows:gain_rows + bias_rows]
    loss = whole[gain_rows + bias_rows:gain_rows + bias_rows + 1]
    loss_out[...] = jnp.sum(loss, axis=-1, keepdims=True)


def tail_call(vec, gain_rows, bias_rows):
    n = lax.axis_size("dp")
    per, owners = slice_rows(gain_rows + bias_rows + 1, n)
    vmem = pl.BlockSpec(memory_space=pltpu.VMEM)
    dma = pltpu.SemaphoreType.DMA
    return pl.pallas_call(
        functools.partial(
            tail_kernel, n, per, owners, gain_rows, bias_rows
        ),
        out_shape=(
            jax.ShapeDtypeStruct((gain_rows, LANES), jnp.float32),
            jax.ShapeDtypeStruct((bias_rows, LANES), jnp.float32),
            jax.ShapeDtypeStruct((1, 1), jnp.float32),
        ),
        in_specs=[vmem],
        out_specs=(vmem,) * 3,
        scratch_shapes=[
            pltpu.VMEM((n - 1, per, LANES), jnp.float32),
            pltpu.VMEM((owners, per, LANES), jnp.float32),
            dma((n - 1,)), dma((n - 1,)),
            dma((n - 1,)), dma((n - 1,)),
        ],
        compiler_params=pltpu.CompilerParams(
            collective_id=0, has_side_effects=True, vmem_limit_bytes=VMEM_LIMIT
        ),
        name="tail",
    )(vec)


def moved(value, steps):
    count = lax.axis_size("dp")
    if steps % count == 0:
        return value
    return lax.ppermute(value, "dp", [(s, (s - steps) % count) for s in range(count)])


def shards(hidden, doc_ids, teacher, rotation, norm_gain_vector, proj_bias, projection):
    members = lax.axis_size("dp")
    here = lax.axis_index("dp")
    turn = rotation[0] % members
    block_rows = hidden.shape[0] * lax.axis_size("tensor")
    overall_rows = block_rows * members
    total_cols = projection.shape[1] * lax.axis_size("tensor")
    gain = norm_gain_vector.reshape(1, -1)
    bias = proj_bias.reshape(-1, LANES)

    digit = min(members, MOST_DIRECT)
    unit = 1
    while unit * digit < members:
        branches = [functools.partial(moved, steps=i * unit) for i in range(digit)]
        teacher = lax.switch((turn // unit) % digit, branches, teacher)
        unit = unit * digit

    row_docs = lax.dynamic_slice_in_dim(doc_ids, here, 1, 0)[0]
    same = jnp.sum((row_docs[:, None] == row_docs[None, :]).astype(jnp.float32), axis=-1)
    weight = jnp.broadcast_to((block_rows / (DOCS * same))[:, None], (block_rows, LANES))
    count = -(-members // unit)
    branches = [functools.partial(block_call, i * unit, 1 + i) for i in range(count)]
    hid, vec = lax.switch(
        turn // unit, branches, hidden, teacher, weight, gain, bias, projection
    )
    gain_sum, bias_sum, loss_sum = tail_call(vec, gain.size // LANES, bias.size // LANES)
    return (
        hid,
        gain_sum.reshape(-1) / overall_rows,
        bias_sum.reshape(-1) / overall_rows,
        loss_sum[0, 0] / (2.0 * overall_rows * total_cols),
    )


def solution(mesh):
    return jax.shard_map(
        shards,
        mesh=mesh,
        in_specs=(
            P(("dp", "tensor"), None),
            P(),
            P("dp", "tensor"),
            P(),
            P(),
            P("tensor"),
            P(None, "tensor"),
        ),
        out_specs=(P(("dp", "tensor"), None), P(), P("tensor"), P()),
        check_vma=False,
    )
```
